32 devices in a mesh: delay: 16 (over z, y, x), row: 2 (over core).
Axes of the slice: x: 2, y: 2, z: 4, core: 2. Of those that a mesh axis runs over, the one named last changes fastest.
Arguments:
- excite: bfloat16 [1, 4096, 128], P(None, 'row'), may hold values from -6 to 6
- present_inverse: bfloat16 [32, 128, 128], P('row'), may hold values from -0.5 to 0.5
- retarded: bfloat16 [16, 32, 16, 128, 128], P('delay', 'row'), may hold values from -0.125 to 0.125
- columns: int32 [16, 32, 16], P('delay', 'row'), may hold values from 0 to 31, as said below
- future_in: float32 [16, 4096, 128], P('delay', 'row'), may hold values from -6 to 6
Outputs:
- currents: bfloat16 [1, 4096, 128], P(None, 'row')
- future_out: float32 [16, 4096, 128], P('delay', 'row')
The draws below stay inside these ranges and needn't reach their ends.
Inputs may be any that keep to these rules, and one draw needn't show every extreme that they name: `columns`: each block row at each delay names 16 different column blocks.
All inputs are finite; a program needn't handle non-finite values.
Results may differ from the reference program's by a relative error of at most 0.0052.
Values may be sent and summed in bfloat16 or wider, within the bound.
No kernel may reach another device: no remote copies, remote signals or barrier semaphores. Data moves between devices by JAX's collectives and lax.ppermute only.
A program may use at most 64 MiB of HBM per device.

```python
import jax
import jax.numpy as jnp
from jax import lax

N_UNK = 4096
BLK = 128
NNZ = 16
EXC = 128
STEPS = 1
DELAYS = 16
BLOCKS = 32


def draw_columns(key, part):
    blocks = N_UNK // BLK
    subkeys = jax.random.split(jax.random.fold_in(key, 7), DELAYS * blocks)

    def pick_order(subkey):
        return jax.random.permutation(subkey, blocks)
    orders = jax.vmap(pick_order)(subkeys)
    return orders[:, :NNZ].reshape(DELAYS, blocks, NNZ).astype(jnp.int32)


def block_levels(key, extent, cuts, smallest, high):
    gain = 1.0
    for dim, shards_of in cuts:
        heights = jax.random.uniform(jax.random.fold_in(jax.random.fold_in(key, 6), dim), (shards_of,), jnp.float32, smallest / len(cuts), high / len(cuts))
        gain = gain * jnp.repeat(jnp.exp(heights), extent[dim] // shards_of).reshape((-1,) + (1,) * (len(extent) - 1 - dim))
    return gain


def bell_draw(own_key, extent, width, most, cuts=(), held_as=jnp.bfloat16):
    result = jax.random.normal(own_key, extent, jnp.float32) * width
    if len(cuts) > 0:
        result = block_levels(own_key, extent, cuts, -0.22, 0.18) * result
    return jnp.clip(result, min=-most, max=most).astype(held_as)


def setup_inputs(seed: int = 0) -> dict:
    keys = jax.random.split(jax.random.key(seed), 6)
    return {
        "excite": bell_draw(keys[0], (STEPS, N_UNK, EXC), 1.0, 6.0, ((1, 2),)),
        "present_inverse": bell_draw(keys[1], (BLOCKS, BLK, BLK), BLK ** -0.5, 0.5, ((0, 2),)),
        "retarded": bell_draw(keys[2], (DELAYS, BLOCKS, NNZ, BLK, BLK), (NNZ * BLK) ** -0.5, 0.125, ((0, 16), (1, 2))),
        "columns": draw_columns(jax.random.fold_in(keys[5], 71), 0),
        "future_in": bell_draw(keys[4], (DELAYS, N_UNK, EXC), 1.0, 6.0, ((0, 16), (1, 2)), jnp.float32),
    }


def reference(excite, present_inverse, retarded, columns, future_in):
    blocks = N_UNK // BLK
    future = future_in
    history = []
    for step in range(STEPS):
        right_side = (excite[step].astype(jnp.float32) - future[0]).astype(jnp.bfloat16)
        stacked = right_side.reshape(blocks, BLK, EXC).astype(jnp.float32)
        solved = jnp.einsum("rab,rbe->rae", present_inverse.astype(jnp.float32), stacked).astype(jnp.bfloat16)
        history.append(solved.reshape(N_UNK, EXC))
        shifted = jnp.concatenate([future[1:], jnp.zeros_like(future[:1])], 0)
        solved_wide = solved.astype(jnp.float32)

        def delay_term(pair):
            weights, indices = pair
            picked = solved_wide[indices.astype(jnp.int32)]
            return jnp.einsum("rkab,rkbe->rae", weights.astype(jnp.float32), picked).reshape(N_UNK, EXC)

        added = lax.map(delay_term, (retarded, columns))
        future = shifted + added
    return jnp.stack(history), future
```

```python
import functools

import jax
import jax.numpy as jnp
from jax import lax
from jax.experimental import pallas as pl
from jax.experimental.pallas import tpu as pltpu
from jax.sharding import PartitionSpec as P

BLK = 128
PLANE = 4

VMEM_SPEC = pl.BlockSpec(memory_space=pltpu.VMEM)
ANY_SPEC = pl.BlockSpec(memory_space=pl.ANY)
SMEM_SPEC = pl.BlockSpec(memory_space=pltpu.SMEM)


def solve_kernel(excite_hbm, inverse_hbm, future_hbm, *refs):
    quarters = refs[:PLANE]
    excite, inverse, future, sems = refs[PLANE:]
    step = quarters[0].shape[0]
    blocks = step // BLK
    root = lax.axis_index("delay") == 0

    def copies(part):
        rows = pl.ds(part * step, step)
        whole = pl.ds(part * blocks, blocks)
        return (
            pltpu.make_async_copy(future_hbm.at[0, rows], future.at[rows], sems.at[0, part]),
            pltpu.make_async_copy(excite_hbm.at[0, rows], excite.at[rows], sems.at[1, part]),
            pltpu.make_async_copy(inverse_hbm.at[whole], inverse.at[whole], sems.at[2, part]),
        )

    @pl.when(root)
    def _():
        for part in reversed(range(PLANE)):
            for copy in copies(part):
                copy.start()
        for part in reversed(range(PLANE)):
            for copy in copies(part):
                copy.wait()
            for block in range(blocks):
                rows = pl.ds(part * step + block * BLK, BLK)
                right = (excite[rows, :].astype(jnp.float32) - future[rows, :]).astype(jnp.bfloat16)
                solved = jnp.dot(
                    inverse[part * blocks + block], right, preferred_element_type=jnp.float32
                )
                quarters[part][pl.ds(block * BLK, BLK), :] = solved.astype(jnp.bfloat16)

    @pl.when(jnp.logical_not(root))
    def _():
        quarters[0][...] = jnp.zeros_like(quarters[0])


def solve(excite, inverse, future):
    rows, width = future.shape[1:]
    quarter = jax.ShapeDtypeStruct((rows // PLANE, width), jnp.bfloat16)
    return pl.pallas_call(
        solve_kernel,
        out_shape=[quarter] * PLANE,
        in_specs=[ANY_SPEC] * 3,
        out_specs=[VMEM_SPEC] * PLANE,
        scratch_shapes=[
            pltpu.VMEM((rows, width), jnp.bfloat16),
            pltpu.VMEM(inverse.shape, jnp.bfloat16),
            pltpu.VMEM((rows, width), jnp.float32),
            pltpu.SemaphoreType.DMA((3, PLANE)),
        ],
    )(excite, inverse, future)


def narrow_kernel(future, out):
    out[...] = future[0].astype(jnp.bfloat16)


def narrow(future):
    rows, width = future.shape[1:]
    return pl.pallas_call(
        narrow_kernel,
        out_shape=jax.ShapeDtypeStruct((rows, width), jnp.bfloat16),
        in_specs=[VMEM_SPEC],
        out_specs=VMEM_SPEC,
    )(future)


def fetch_kernel(weights_hbm, out, sem):
    copy = pltpu.make_async_copy(weights_hbm.at[0], out, sem)
    copy.start()
    copy.wait()


def fetch(weights):
    return pl.pallas_call(
        fetch_kernel,
        out_shape=jax.ShapeDtypeStruct(weights.shape[1:], weights.dtype),
        in_specs=[ANY_SPEC],
        out_specs=VMEM_SPEC,
        scratch_shapes=[pltpu.SemaphoreType.DMA],
        compiler_params=pltpu.CompilerParams(vmem_limit_bytes=40 << 20),
    )(weights)


def product_kernel(halves, columns, weights, shifted, *refs):
    pieces = refs[: halves * PLANE]
    currents_hbm, future_hbm, whole, total, sems = refs[halves * PLANE :]
    step = pieces[0].shape[0] // BLK
    row_blocks, slots = weights.shape[:2]
    mine = lax.rem(lax.axis_index("delay"), PLANE)
    row = lax.axis_index("row")
    for turn in range(halves):
        half = lax.rem(row - turn + halves, halves)
        for mask in range(PLANE):
            start = (half * PLANE + lax.bitwise_xor(mine, mask)) * step
            piece = pieces[turn * PLANE + mask]
            for block in range(step):
                whole[start + block] = piece[pl.ds(block * BLK, BLK), :]

    own = pltpu.make_async_copy(
        whole.at[pl.ds(row * row_blocks, row_blocks)], currents_hbm, sems.at[row_blocks]
    )
    own.start()

    def out_copy(r):
        rows = pl.ds(r * BLK, BLK)
        return pltpu.make_async_copy(total.at[rows], future_hbm.at[rows], sems.at[r])

    def one_row(r, carry):
        left = jnp.concatenate([weights[r, k] for k in range(slots)], axis=1)
        right = jnp.concatenate([whole[columns[0, r, k]] for k in range(slots)], axis=0)
        rows = pl.ds(pl.multiple_of(r * BLK, BLK), BLK)
        added = jnp.dot(left, right, preferred_element_type=jnp.float32)
        total[rows, :] = shifted[rows, :].astype(jnp.float32) + added
        out_copy(r).start()
        return carry

    lax.fori_loop(0, row_blocks, one_row, 0)
    own.wait()

    def one_wait(r, carry):
        out_copy(r).wait()
        return carry

    lax.fori_loop(0, row_blocks, one_wait, 0)


def product(columns, weights, shifted, pieces, halves):
    row_blocks = weights.shape[0]
    rows, width = shifted.shape
    return pl.pallas_call(
        functools.partial(product_kernel, halves),
        out_shape=[
            jax.ShapeDtypeStruct((row_blocks, BLK, width), jnp.bfloat16),
            jax.ShapeDtypeStruct((rows, width), jnp.float32),
        ],
        in_specs=[SMEM_SPEC, VMEM_SPEC, VMEM_SPEC] + [VMEM_SPEC] * len(pieces),
        out_specs=[ANY_SPEC, ANY_SPEC],
        scratch_shapes=[
            pltpu.VMEM((halves * row_blocks, BLK, width), jnp.bfloat16),
            pltpu.VMEM((rows, width), jnp.float32),
            pltpu.SemaphoreType.DMA((row_blocks + 1,)),
        ],
        compiler_params=pltpu.CompilerParams(vmem_limit_bytes=40 << 20),
    )(columns, weights, shifted, *pieces)


def per_device(excite, present_inverse, retarded, columns, future_in):
    delays, halves = lax.axis_size("delay"), lax.axis_size("row")
    planes = delays // PLANE
    rows, width = future_in.shape[1:]

    quarters = solve(excite, present_inverse, future_in)
    spread = [lax.ppermute(quarters[k], "delay", [(0, k)]) for k in (3, 2, 1)]
    weights, narrowed = fetch(retarded), narrow(future_in)
    spread, weights, narrowed = lax.optimization_barrier((spread, weights, narrowed))
    shifted = lax.ppermute(narrowed, "delay", [(i, i - 1) for i in range(1, delays)])
    piece = quarters[0] + spread[0] + spread[1] + spread[2]
    reach = planes
    while reach > 1:
        reach //= 2
        pairs = [
            (z * PLANE + q, (z + reach) * PLANE + q)
            for z in range(0, planes, 2 * reach)
            for q in range(PLANE)
        ]
        piece = piece + lax.ppermute(piece, "delay", pairs)
    held = [piece] + [None] * (PLANE - 1)
    for mask in (3, 1, 2):
        held[mask] = lax.ppermute(piece, "delay", [(i, i ^ mask) for i in range(delays)])
    pieces = list(held)
    for turn in range(1, halves):
        pairs = [(i, (i + turn) % halves) for i in range(halves)]
        pieces += [lax.ppermute(p, "row", pairs) for p in held]
    currents, future = product(columns, weights, shifted, pieces, halves)
    return currents.reshape(1, rows, width), future[None]


def solution(mesh):
    return jax.shard_map(
        per_device,
        mesh=mesh,
        in_specs=(
            P(None, "row", None),
            P("row", None, None),
            P("delay", "row", None, None, None),
            P("delay", "row", None),
            P("delay", "row", None),
        ),
        out_specs=(P(None, "row", None), P("delay", "row", None)),
        check_vma=False,
    )
```

```python
import functools

import jax
import jax.numpy as jnp
from jax import lax
from jax.experimental import pallas as pl
from jax.experimental.pallas import tpu as pltpu
from jax.sharding import PartitionSpec as P

BLK = 128
PLANE = 4

VMEM_SPEC = pl.BlockSpec(memory_space=pltpu.VMEM)
ANY_SPEC = pl.BlockSpec(memory_space=pl.ANY)
SMEM_SPEC = pl.BlockSpec(memory_space=pltpu.SMEM)


def solve_kernel(excite_hbm, inverse_hbm, future_hbm, *refs):
    quarters = refs[:PLANE]
    excite, inverse, future, sems = refs[PLANE:]
    step = quarters[0].shape[0]
    blocks = step // BLK
    root = lax.axis_index("delay") == 0

    def copies(part):
        rows = pl.ds(part * step, step)
        whole = pl.ds(part * blocks, blocks)
        return (
            pltpu.make_async_copy(future_hbm.at[0, rows], future.at[rows], sems.at[0, part]),
            pltpu.make_async_copy(excite_hbm.at[0, rows], excite.at[rows], sems.at[1, part]),
            pltpu.make_async_copy(inverse_hbm.at[whole], inverse.at[whole], sems.at[2, part]),
        )

    @pl.when(root)
    def _():
        for part in reversed(range(PLANE)):
            for copy in copies(part):
                copy.start()
        for part in reversed(range(PLANE)):
            for copy in copies(part):
                copy.wait()
            for block in range(blocks):
                rows = pl.ds(part * step + block * BLK, BLK)
                right = (excite[rows, :].astype(jnp.float32) - future[rows, :]).astype(jnp.bfloat16)
                solved = jnp.dot(
                    inverse[part * blocks + block], right, preferred_element_type=jnp.float32
                )
                quarters[part][pl.ds(block * BLK, BLK), :] = solved.astype(jnp.bfloat16)

    @pl.when(jnp.logical_not(root))
    def _():
        quarters[0][...] = jnp.zeros_like(quarters[0])


def solve(excite, inverse, future):
    rows, width = future.shape[1:]
    quarter = pltpu.VMEM((rows // PLANE, width), jnp.bfloat16)
    return pl.pallas_call(
        solve_kernel,
        out_shape=[quarter] * PLANE,
        in_specs=[ANY_SPEC] * 3,
        out_specs=[VMEM_SPEC] * PLANE,
        scratch_shapes=[
            pltpu.VMEM((rows, width), jnp.bfloat16),
            pltpu.VMEM(inverse.shape, jnp.bfloat16),
            pltpu.VMEM((rows, width), jnp.float32),
            pltpu.SemaphoreType.DMA((3, PLANE)),
        ],
    )(excite, inverse, future)


def narrow_kernel(parts, future_hbm, out, future, sems):
    step = future.shape[0] // parts

    def copy(part):
        rows = pl.ds(part * step, step)
        return pltpu.make_async_copy(future_hbm.at[0, rows], future.at[rows], sems.at[part])

    for part in range(parts):
        copy(part).start()
    for part in range(parts):
        copy(part).wait()
        rows = pl.ds(part * step, step)
        out[rows, :] = future[rows, :].astype(jnp.bfloat16)


def narrow(future):
    rows, width = future.shape[1:]
    return pl.pallas_call(
        functools.partial(narrow_kernel, PLANE),
        out_shape=pltpu.VMEM((rows, width), jnp.bfloat16),
        in_specs=[ANY_SPEC],
        out_specs=VMEM_SPEC,
        scratch_shapes=[
            pltpu.VMEM((rows, width), jnp.float32),
            pltpu.SemaphoreType.DMA((PLANE,)),
        ],
    )(future)


def fetch_kernel(first, weights_hbm, out, sem):
    copy = pltpu.make_async_copy(weights_hbm.at[0, pl.ds(first, out.shape[0])], out, sem)
    copy.start()
    copy.wait()


def fetch(weights, first, count):
    return pl.pallas_call(
        functools.partial(fetch_kernel, first),
        out_shape=jax.ShapeDtypeStruct((count,) + weights.shape[2:], weights.dtype),
        in_specs=[ANY_SPEC],
        out_specs=VMEM_SPEC,
        scratch_shapes=[pltpu.SemaphoreType.DMA],
        compiler_params=pltpu.CompilerParams(vmem_limit_bytes=40 << 20),
    )(pltpu.with_memory_space_constraint(weights, pltpu.HBM))


def product_kernel(halves, columns, first_weights, other_weights, shifted, *refs):
    pieces = refs[: halves * PLANE]
    currents_hbm, future_hbm, whole, total, sems = refs[halves * PLANE :]
    step = pieces[0].shape[0] // BLK
    row_blocks, slots = columns.shape[1:]
    cut = first_weights.shape[0]
    mine = lax.rem(lax.axis_index("delay"), PLANE)
    row = lax.axis_index("row")
    for turn in range(halves):
        half = lax.rem(row - turn + halves, halves)
        for mask in range(PLANE):
            start = (half * PLANE + lax.bitwise_xor(mine, mask)) * step
            piece = pieces[turn * PLANE + mask]
            for block in range(step):
                whole[start + block] = piece[pl.ds(block * BLK, BLK), :]

    own = pltpu.make_async_copy(
        whole.at[pl.ds(row * row_blocks, row_blocks)], currents_hbm, sems.at[row_blocks]
    )
    own.start()

    def out_copy(r):
        rows = pl.ds(r * BLK, BLK)
        return pltpu.make_async_copy(total.at[rows], future_hbm.at[rows], sems.at[r])

    for r in range(row_blocks):
        weights, at = (first_weights, r) if r < cut else (other_weights, r - cut)
        left = jnp.concatenate([weights[at, k] for k in range(slots)], axis=1)
        right = jnp.concatenate([whole[columns[0, r, k]] for k in range(slots)], axis=0)
        rows = pl.ds(r * BLK, BLK)
        added = jnp.dot(left, right, preferred_element_type=jnp.float32)
        total[rows, :] = shifted[rows, :].astype(jnp.float32) + added
        out_copy(r).start()
    own.wait()
    for r in range(row_blocks):
        out_copy(r).wait()


def product(columns, weights, shifted, pieces, halves):
    row_blocks = columns.shape[1]
    rows, width = shifted.shape
    return pl.pallas_call(
        functools.partial(product_kernel, halves),
        out_shape=[
            jax.ShapeDtypeStruct((row_blocks, BLK, width), jnp.bfloat16),
            jax.ShapeDtypeStruct((rows, width), jnp.float32),
        ],
        in_specs=[SMEM_SPEC] + [VMEM_SPEC] * (3 + len(pieces)),
        out_specs=[ANY_SPEC, ANY_SPEC],
        scratch_shapes=[
            pltpu.VMEM((halves * row_blocks, BLK, width), jnp.bfloat16),
            pltpu.VMEM((rows, width), jnp.float32),
            pltpu.SemaphoreType.DMA((row_blocks + 1,)),
        ],
        compiler_params=pltpu.CompilerParams(vmem_limit_bytes=40 << 20),
    )(columns, *weights, shifted, *pieces)


def per_device(excite, present_inverse, retarded, columns, future_in):
    delays, halves = lax.axis_size("delay"), lax.axis_size("row")
    planes = delays // PLANE
    rows, width = future_in.shape[1:]

    quarters = solve(excite, present_inverse, future_in)
    spread = [lax.ppermute(quarters[k], "delay", [(0, k)]) for k in (3, 2, 1)]
    narrowed = narrow(future_in)
    half_rows = columns.shape[1] // 2
    first_weights = fetch(retarded, 0, half_rows)
    spread, first_weights, narrowed = lax.optimization_barrier((spread, first_weights, narrowed))
    shifted = lax.ppermute(narrowed, "delay", [(i, i - 1) for i in range(1, delays)])
    piece = quarters[0] + spread[0] + spread[1] + spread[2]
    reach = planes
    while reach > 1:
        reach //= 2
        pairs = [
            (z * PLANE + q, (z + reach) * PLANE + q)
            for z in range(0, planes, 2 * reach)
            for q in range(PLANE)
        ]
        piece = piece + lax.ppermute(piece, "delay", pairs)
    other_weights = fetch(retarded, half_rows, half_rows)
    piece, other_weights = lax.optimization_barrier((piece, other_weights))
    held = [piece] + [None] * (PLANE - 1)
    for mask in (3, 1, 2):
        held[mask] = lax.ppermute(piece, "delay", [(i, i ^ mask) for i in range(delays)])
    pieces = list(held)
    for turn in range(1, halves):
        pairs = [(i, (i + turn) % halves) for i in range(halves)]
        pieces += [lax.ppermute(p, "row", pairs) for p in held]
    currents, future = product(
        columns, (first_weights, other_weights), shifted, pieces, halves
    )
    return currents.reshape(1, rows, width), future[None]


def solution(mesh):
    return jax.shard_map(
        per_device,
        mesh=mesh,
        in_specs=(
            P(None, "row", None),
            P("row", None, None),
            P("delay", "row", None, None, None),
            P("delay", "row", None),
            P("delay", "row", None),
        ),
        out_specs=(P(None, "row", None), P("delay", "row", None)),
        check_vma=False,
    )
```

```python
import functools

import jax
import jax.numpy as jnp
from jax import lax
from jax.experimental import pallas as pl
from jax.experimental.pallas import tpu as pltpu
from jax.sharding import PartitionSpec as P

BLK = 128
PLANE = 4

VMEM_SPEC = pl.BlockSpec(memory_space=pltpu.VMEM)
ANY_SPEC = pl.BlockSpec(memory_space=pl.ANY)
SMEM_SPEC = pl.BlockSpec(memory_space=pltpu.SMEM)


def solve_kernel(excite_hbm, inverse_hbm, future_hbm, *refs):
    quarters = refs[:PLANE]
    excite, inverse, future, sems = refs[PLANE:]
    step = quarters[0].shape[0]
    blocks = step // BLK
    root = lax.axis_index("delay") == 0

    def copies(part):
        rows = pl.ds(part * step, step)
        whole = pl.ds(part * blocks, blocks)
        return (
            pltpu.make_async_copy(future_hbm.at[0, rows], future.at[rows], sems.at[0, part]),
            pltpu.make_async_copy(excite_hbm.at[0, rows], excite.at[rows], sems.at[1, part]),
            pltpu.make_async_copy(inverse_hbm.at[whole], inverse.at[whole], sems.at[2, part]),
        )

    @pl.when(root)
    def _():
        for part in reversed(range(PLANE)):
            for copy in copies(part):
                copy.start()
        for part in reversed(range(PLANE)):
            for copy in copies(part):
                copy.wait()
            for block in range(blocks):
                rows = pl.ds(part * step + block * BLK, BLK)
                right = (excite[rows, :].astype(jnp.float32) - future[rows, :]).astype(jnp.bfloat16)
                solved = jnp.dot(
                    inverse[part * blocks + block], right, preferred_element_type=jnp.float32
                )
                quarters[part][pl.ds(block * BLK, BLK), :] = solved.astype(jnp.bfloat16)

    @pl.when(jnp.logical_not(root))
    def _():
        quarters[0][...] = jnp.zeros_like(quarters[0])


def solve(excite, inverse, future):
    rows, width = future.shape[1:]
    quarter = pltpu.VMEM((rows // PLANE, width), jnp.bfloat16)
    return pl.pallas_call(
        solve_kernel,
        out_shape=[quarter] * PLANE,
        in_specs=[ANY_SPEC] * 3,
        out_specs=[VMEM_SPEC] * PLANE,
        scratch_shapes=[
            pltpu.VMEM((rows, width), jnp.bfloat16),
            pltpu.VMEM(inverse.shape, jnp.bfloat16),
            pltpu.VMEM((rows, width), jnp.float32),
            pltpu.SemaphoreType.DMA((3, PLANE)),
        ],
    )(excite, inverse, future)


def narrow_kernel(parts, future_hbm, out, future, sems):
    step = future.shape[0] // parts

    def copy(part):
        rows = pl.ds(part * step, step)
        return pltpu.make_async_copy(future_hbm.at[0, rows], future.at[rows], sems.at[part])

    for part in range(parts):
        copy(part).start()
    for part in range(parts):
        copy(part).wait()
        rows = pl.ds(part * step, step)
        out[rows, :] = future[rows, :].astype(jnp.bfloat16)


def narrow(future):
    rows, width = future.shape[1:]
    return pl.pallas_call(
        functools.partial(narrow_kernel, PLANE),
        out_shape=pltpu.VMEM((rows, width), jnp.bfloat16),
        in_specs=[ANY_SPEC],
        out_specs=VMEM_SPEC,
        scratch_shapes=[
            pltpu.VMEM((rows, width), jnp.float32),
            pltpu.SemaphoreType.DMA((PLANE,)),
        ],
    )(future)


def fetch_kernel(first, weights_hbm, out, sem):
    copy = pltpu.make_async_copy(weights_hbm.at[0, pl.ds(first, out.shape[0])], out, sem)
    copy.start()
    copy.wait()


def fetch(weights, first, count):
    return pl.pallas_call(
        functools.partial(fetch_kernel, first),
        out_shape=jax.ShapeDtypeStruct((count,) + weights.shape[2:], weights.dtype),
        in_specs=[ANY_SPEC],
        out_specs=VMEM_SPEC,
        scratch_shapes=[pltpu.SemaphoreType.DMA],
        compiler_params=pltpu.CompilerParams(vmem_limit_bytes=40 << 20),
    )(pltpu.with_memory_space_constraint(weights, pltpu.HBM))


def product_kernel(halves, columns, first_weights, other_weights, shifted, *refs):
    pieces = refs[: halves * PLANE]
    currents_hbm, future_hbm, whole, total, sems = refs[halves * PLANE :]
    step = pieces[0].shape[0] // BLK
    row_blocks, slots = columns.shape[1:]
    cut = first_weights.shape[0]
    mine = lax.rem(lax.axis_index("delay"), PLANE)
    row = lax.axis_index("row")
    for turn in range(halves):
        half = lax.rem(row - turn + halves, halves)
        for mask in range(PLANE):
            start = (half * PLANE + lax.bitwise_xor(mine, mask)) * step
            piece = pieces[turn * PLANE + mask]
            for block in range(step):
                whole[start + block] = piece[pl.ds(block * BLK, BLK), :]

    own = pltpu.make_async_copy(
        whole.at[pl.ds(row * row_blocks, row_blocks)], currents_hbm, sems.at[row_blocks]
    )
    own.start()

    def out_copy(r):
        rows = pl.ds(r * BLK, BLK)
        return pltpu.make_async_copy(total.at[rows], future_hbm.at[rows], sems.at[r])

    for r in range(row_blocks):
        weights, at = (first_weights, r) if r < cut else (other_weights, r - cut)
        left = jnp.concatenate([weights[at, k] for k in range(slots)], axis=1)
        right = jnp.concatenate([whole[columns[0, r, k]] for k in range(slots)], axis=0)
        rows = pl.ds(r * BLK, BLK)
        added = jnp.dot(left, right, preferred_element_type=jnp.float32)
        total[rows, :] = shifted[rows, :].astype(jnp.float32) + added
        out_copy(r).start()
    own.wait()
    for r in range(row_blocks):
        out_copy(r).wait()


def product(columns, weights, shifted, pieces, halves):
    row_blocks = columns.shape[1]
    rows, width = shifted.shape
    return pl.pallas_call(
        functools.partial(product_kernel, halves),
        out_shape=[
            jax.ShapeDtypeStruct((row_blocks, BLK, width), jnp.bfloat16),
            jax.ShapeDtypeStruct((rows, width), jnp.float32),
        ],
        in_specs=[SMEM_SPEC] + [VMEM_SPEC] * (3 + len(pieces)),
        out_specs=[ANY_SPEC, ANY_SPEC],
        scratch_shapes=[
            pltpu.VMEM((halves * row_blocks, BLK, width), jnp.bfloat16),
            pltpu.VMEM((rows, width), jnp.float32),
            pltpu.SemaphoreType.DMA((row_blocks + 1,)),
        ],
        compiler_params=pltpu.CompilerParams(vmem_limit_bytes=40 << 20),
    )(columns, *weights, shifted, *pieces)


def per_device(excite, present_inverse, retarded, columns, future_in):
    delays, halves = lax.axis_size("delay"), lax.axis_size("row")
    planes = delays // PLANE
    rows, width = future_in.shape[1:]

    quarters = solve(excite, present_inverse, future_in)
    spread = [lax.ppermute(quarters[k], "delay", [(0, k)]) for k in (3, 2, 1)]
    narrowed = narrow(future_in)
    half_rows = columns.shape[1] // 2
    first_weights = fetch(retarded, 0, half_rows)
    spread, first_weights, narrowed = lax.optimization_barrier((spread, first_weights, narrowed))
    shifted = lax.ppermute(narrowed, "delay", [(i, i - 1) for i in range(1, delays)])
    piece = quarters[0] + spread[0] + spread[1] + spread[2]
    reach = planes
    while reach > 1:
        reach //= 2
        pairs = [
            (z * PLANE + q, (z + reach) * PLANE + q)
            for z in range(0, planes, 2 * reach)
            for q in range(PLANE)
        ]
        piece = piece + lax.ppermute(piece, "delay", pairs)
    other_weights = fetch(retarded, half_rows, half_rows)
    piece, other_weights = lax.optimization_barrier((piece, other_weights))
    held = [piece] + [None] * (PLANE - 1)
    for mask in (3, 1, 2):
        held[mask] = lax.ppermute(piece, "delay", [(i, i ^ mask) for i in range(delays)])
    held[3], shifted = lax.optimization_barrier((held[3], shifted))
    pieces = list(held)
    for turn in range(1, halves):
        pairs = [(i, (i + turn) % halves) for i in range(halves)]
        pieces += [lax.ppermute(p, "row", pairs) for p in held]
    currents, future = product(
        columns, (first_weights, other_weights), shifted, pieces, halves
    )
    return currents.reshape(1, rows, width), future[None]


def solution(mesh):
    return jax.shard_map(
        per_device,
        mesh=mesh,
        in_specs=(
            P(None, "row", None),
            P("row", None, None),
            P("delay", "row", None, None, None),
            P("delay", "row", None),
            P("delay", "row", None),
        ),
        out_specs=(P(None, "row", None), P("delay", "row", None)),
        check_vma=False,
    )
```

```python
import functools

import jax
import jax.numpy as jnp
from jax import lax
from jax.experimental import pallas as pl
from jax.experimental.pallas import tpu as pltpu
from jax.sharding import PartitionSpec as P

BLK = 128
PLANE = 4

VMEM_SPEC = pl.BlockSpec(memory_space=pltpu.VMEM)
ANY_SPEC = pl.BlockSpec(memory_space=pl.ANY)
SMEM_SPEC = pl.BlockSpec(memory_space=pltpu.SMEM)


def solve_kernel(excite_hbm, inverse_hbm, future_hbm, *refs):
    quarters = refs[:PLANE]
    excite, inverse, future, sems = refs[PLANE:]
    step = quarters[0].shape[0]
    blocks = step // BLK
    root = lax.axis_index("delay") == 0

    def copies(part):
        rows = pl.ds(part * step, step)
        whole = pl.ds(part * blocks, blocks)
        return (
            pltpu.make_async_copy(future_hbm.at[0, rows], future.at[rows], sems.at[0, part]),
            pltpu.make_async_copy(excite_hbm.at[0, rows], excite.at[rows], sems.at[1, part]),
            pltpu.make_async_copy(inverse_hbm.at[whole], inverse.at[whole], sems.at[2, part]),
        )

    @pl.when(root)
    def _():
        for part in reversed(range(PLANE)):
            for copy in copies(part):
                copy.start()
        for part in reversed(range(PLANE)):
            for copy in copies(part):
                copy.wait()
            for block in range(blocks):
                rows = pl.ds(part * step + block * BLK, BLK)
                right = (excite[rows, :].astype(jnp.float32) - future[rows, :]).astype(jnp.bfloat16)
                solved = jnp.dot(
                    inverse[part * blocks + block], right, preferred_element_type=jnp.float32
                )
                quarters[part][pl.ds(block * BLK, BLK), :] = solved.astype(jnp.bfloat16)

    @pl.when(jnp.logical_not(root))
    def _():
        quarters[0][...] = jnp.zeros_like(quarters[0])


def solve(excite, inverse, future):
    rows, width = future.shape[1:]
    quarter = pltpu.VMEM((rows // PLANE, width), jnp.bfloat16)
    return pl.pallas_call(
        solve_kernel,
        out_shape=[quarter] * PLANE,
        in_specs=[ANY_SPEC] * 3,
        out_specs=[VMEM_SPEC] * PLANE,
        scratch_shapes=[
            pltpu.VMEM((rows, width), jnp.bfloat16),
            pltpu.VMEM(inverse.shape, jnp.bfloat16),
            pltpu.VMEM((rows, width), jnp.float32),
            pltpu.SemaphoreType.DMA((3, PLANE)),
        ],
    )(excite, inverse, future)


def narrow_kernel(parts, future_hbm, out, future, sems):
    step = future.shape[0] // parts

    def copy(part):
        rows = pl.ds(part * step, step)
        return pltpu.make_async_copy(future_hbm.at[0, rows], future.at[rows], sems.at[part])

    for part in range(parts):
        copy(part).start()
    for part in range(parts):
        copy(part).wait()
        rows = pl.ds(part * step, step)
        out[rows, :] = future[rows, :].astype(jnp.bfloat16)


def narrow(future):
    rows, width = future.shape[1:]
    return pl.pallas_call(
        functools.partial(narrow_kernel, PLANE),
        out_shape=pltpu.VMEM((rows, width), jnp.bfloat16),
        in_specs=[ANY_SPEC],
        out_specs=VMEM_SPEC,
        scratch_shapes=[
            pltpu.VMEM((rows, width), jnp.float32),
            pltpu.SemaphoreType.DMA((PLANE,)),
        ],
    )(future)


def fetch_kernel(first, weights_hbm, out, sem):
    copy = pltpu.make_async_copy(weights_hbm.at[0, pl.ds(first, out.shape[0])], out, sem)
    copy.start()
    copy.wait()


def fetch(weights, first, count):
    return pl.pallas_call(
        functools.partial(fetch_kernel, first),
        out_shape=jax.ShapeDtypeStruct((count,) + weights.shape[2:], weights.dtype),
        in_specs=[ANY_SPEC],
        out_specs=VMEM_SPEC,
        scratch_shapes=[pltpu.SemaphoreType.DMA],
        compiler_params=pltpu.CompilerParams(vmem_limit_bytes=40 << 20),
    )(pltpu.with_memory_space_constraint(weights, pltpu.HBM))


def product_kernel(halves, columns, first_weights, other_weights, shifted, *refs):
    pieces = refs[: halves * PLANE]
    currents_hbm, future_hbm, whole, total, sems = refs[halves * PLANE :]
    step = pieces[0].shape[0] // BLK
    row_blocks, slots = columns.shape[1:]
    cut = first_weights.shape[0]
    mine = lax.rem(lax.axis_index("delay"), PLANE)
    row = lax.axis_index("row")
    for turn in range(halves):
        half = lax.rem(row - turn + halves, halves)
        for mask in range(PLANE):
            start = (half * PLANE + lax.bitwise_xor(mine, mask)) * step
            piece = pieces[turn * PLANE + mask]
            for block in range(step):
                whole[start + block] = piece[pl.ds(block * BLK, BLK), :]

    own = pltpu.make_async_copy(
        whole.at[pl.ds(row * row_blocks, row_blocks)], currents_hbm, sems.at[row_blocks]
    )
    own.start()

    def out_copy(r):
        rows = pl.ds(r * BLK, BLK)
        return pltpu.make_async_copy(total.at[rows], future_hbm.at[rows], sems.at[r])

    for r in range(row_blocks):
        weights, at = (first_weights, r) if r < cut else (other_weights, r - cut)
        left = jnp.concatenate([weights[at, k] for k in range(slots)], axis=1)
        right = jnp.concatenate([whole[columns[0, r, k]] for k in range(slots)], axis=0)
        rows = pl.ds(r * BLK, BLK)
        added = jnp.dot(left, right, preferred_element_type=jnp.float32)
        total[rows, :] = shifted[rows, :].astype(jnp.float32) + added
        out_copy(r).start()
    own.wait()
    for r in range(row_blocks):
        out_copy(r).wait()


def product(columns, weights, shifted, pieces, halves):
    row_blocks = columns.shape[1]
    rows, width = shifted.shape
    return pl.pallas_call(
        functools.partial(product_kernel, halves),
        out_shape=[
            jax.ShapeDtypeStruct((row_blocks, BLK, width), jnp.bfloat16),
            jax.ShapeDtypeStruct((rows, width), jnp.float32),
        ],
        in_specs=[SMEM_SPEC] + [VMEM_SPEC] * (3 + len(pieces)),
        out_specs=[ANY_SPEC, ANY_SPEC],
        scratch_shapes=[
            pltpu.VMEM((halves * row_blocks, BLK, width), jnp.bfloat16),
            pltpu.VMEM((rows, width), jnp.float32),
            pltpu.SemaphoreType.DMA((row_blocks + 1,)),
        ],
        compiler_params=pltpu.CompilerParams(vmem_limit_bytes=40 << 20),
    )(columns, *weights, shifted, *pieces)


def per_device(excite, present_inverse, retarded, columns, future_in):
    delays, halves = lax.axis_size("delay"), lax.axis_size("row")
    planes = delays // PLANE
    rows, width = future_in.shape[1:]

    quarters = solve(excite, present_inverse, future_in)
    spread = [lax.ppermute(quarters[k], "delay", [(0, k)]) for k in (3, 2, 1)]
    narrowed = narrow(future_in)
    half_rows = columns.shape[1] // 2
    first_weights = fetch(retarded, 0, half_rows)
    spread[0], first_weights, narrowed = lax.optimization_barrier((spread[0], first_weights, narrowed))
    shifted = lax.ppermute(narrowed, "delay", [(i, i - 1) for i in range(1, delays)])
    piece = quarters[0] + spread[0] + spread[1] + spread[2]
    reach = planes
    while reach > 1:
        reach //= 2
        pairs = [
            (z * PLANE + q, (z + reach) * PLANE + q)
            for z in range(0, planes, 2 * reach)
            for q in range(PLANE)
        ]
        piece = piece + lax.ppermute(piece, "delay", pairs)
    other_weights = fetch(retarded, half_rows, half_rows)
    piece, other_weights = lax.optimization_barrier((piece, other_weights))
    held = [piece] + [None] * (PLANE - 1)
    for mask in (3, 1, 2):
        held[mask] = lax.ppermute(piece, "delay", [(i, i ^ mask) for i in range(delays)])
    held[3], shifted = lax.optimization_barrier((held[3], shifted))
    pieces = list(held)
    for turn in range(1, halves):
        pairs = [(i, (i + turn) % halves) for i in range(halves)]
        pieces += [lax.ppermute(p, "row", pairs) for p in held]
    currents, future = product(
        columns, (first_weights, other_weights), shifted, pieces, halves
    )
    return currents.reshape(1, rows, width), future[None]


def solution(mesh):
    return jax.shard_map(
        per_device,
        mesh=mesh,
        in_specs=(
            P(None, "row", None),
            P("row", None, None),
            P("delay", "row", None, None, None),
            P("delay", "row", None),
            P("delay", "row", None),
        ),
        out_specs=(P(None, "row", None), P("delay", "row", None)),
        check_vma=False,
    )
```

```python
import functools

import jax
import jax.numpy as jnp
from jax import lax
from jax.experimental import pallas as pl
from jax.experimental.pallas import tpu as pltpu
from jax.sharding import PartitionSpec as P

BLK = 128
PLANE = 4

VMEM_SPEC = pl.BlockSpec(memory_space=pltpu.VMEM)
ANY_SPEC = pl.BlockSpec(memory_space=pl.ANY)
SMEM_SPEC = pl.BlockSpec(memory_space=pltpu.SMEM)


def solve_kernel(excite_hbm, inverse_hbm, future_hbm, *refs):
    quarters = refs[:PLANE]
    excite, inverse, future, sems = refs[PLANE:]
    step = quarters[0].shape[0]
    blocks = step // BLK
    root = lax.axis_index("delay") == 0

    def copies(part):
        rows = pl.ds(part * step, step)
        whole = pl.ds(part * blocks, blocks)
        return (
            pltpu.make_async_copy(future_hbm.at[0, rows], future.at[rows], sems.at[0, part]),
            pltpu.make_async_copy(excite_hbm.at[0, rows], excite.at[rows], sems.at[1, part]),
            pltpu.make_async_copy(inverse_hbm.at[whole], inverse.at[whole], sems.at[2, part]),
        )

    @pl.when(root)
    def _():
        for part in reversed(range(PLANE)):
            for copy in copies(part):
                copy.start()
        for part in reversed(range(PLANE)):
            for copy in copies(part):
                copy.wait()
            for block in range(blocks):
                rows = pl.ds(part * step + block * BLK, BLK)
                right = (excite[rows, :].astype(jnp.float32) - future[rows, :]).astype(jnp.bfloat16)
                solved = jnp.dot(
                    inverse[part * blocks + block], right, preferred_element_type=jnp.float32
                )
                quarters[part][pl.ds(block * BLK, BLK), :] = solved.astype(jnp.bfloat16)

    @pl.when(jnp.logical_not(root))
    def _():
        quarters[0][...] = jnp.zeros_like(quarters[0])


def solve(excite, inverse, future):
    rows, width = future.shape[1:]
    quarter = pltpu.VMEM((rows // PLANE, width), jnp.bfloat16)
    return pl.pallas_call(
        solve_kernel,
        out_shape=[quarter] * PLANE,
        in_specs=[ANY_SPEC] * 3,
        out_specs=[VMEM_SPEC] * PLANE,
        scratch_shapes=[
            pltpu.VMEM((rows, width), jnp.bfloat16),
            pltpu.VMEM(inverse.shape, jnp.bfloat16),
            pltpu.VMEM((rows, width), jnp.float32),
            pltpu.SemaphoreType.DMA((3, PLANE)),
        ],
    )(excite, inverse, future)


def narrow_kernel(parts, future_hbm, out, future, sems):
    step = future.shape[0] // parts

    def copy(part):
        rows = pl.ds(part * step, step)
        return pltpu.make_async_copy(future_hbm.at[0, rows], future.at[rows], sems.at[part])

    for part in range(parts):
        copy(part).start()
    for part in range(parts):
        copy(part).wait()
        rows = pl.ds(part * step, step)
        out[rows, :] = future[rows, :].astype(jnp.bfloat16)


def narrow(future):
    rows, width = future.shape[1:]
    return pl.pallas_call(
        functools.partial(narrow_kernel, PLANE),
        out_shape=pltpu.VMEM((rows, width), jnp.bfloat16),
        in_specs=[ANY_SPEC],
        out_specs=VMEM_SPEC,
        scratch_shapes=[
            pltpu.VMEM((rows, width), jnp.float32),
            pltpu.SemaphoreType.DMA((PLANE,)),
        ],
    )(future)


def fetch_kernel(first, weights_hbm, out, sem):
    copy = pltpu.make_async_copy(weights_hbm.at[0, pl.ds(first, out.shape[0])], out, sem)
    copy.start()
    copy.wait()


def fetch(weights, first, count):
    return pl.pallas_call(
        functools.partial(fetch_kernel, first),
        out_shape=jax.ShapeDtypeStruct((count,) + weights.shape[2:], weights.dtype),
        in_specs=[ANY_SPEC],
        out_specs=VMEM_SPEC,
        scratch_shapes=[pltpu.SemaphoreType.DMA],
        compiler_params=pltpu.CompilerParams(vmem_limit_bytes=40 << 20),
    )(pltpu.with_memory_space_constraint(weights, pltpu.HBM))


def product_kernel(halves, columns, first_weights, other_weights, shifted, *refs):
    pieces = refs[: halves * PLANE]
    currents_hbm, future_hbm, whole, total, sems = refs[halves * PLANE :]
    step = pieces[0].shape[0] // BLK
    row_blocks, slots = columns.shape[1:]
    cut = first_weights.shape[0]
    mine = lax.rem(lax.axis_index("delay"), PLANE)
    row = lax.axis_index("row")
    for turn in range(halves):
        half = lax.rem(row - turn + halves, halves)
        for mask in range(PLANE):
            start = (half * PLANE + lax.bitwise_xor(mine, mask)) * step
            piece = pieces[turn * PLANE + mask]
            for block in range(step):
                whole[start + block] = piece[pl.ds(block * BLK, BLK), :]

    own = pltpu.make_async_copy(
        whole.at[pl.ds(row * row_blocks, row_blocks)], currents_hbm, sems.at[row_blocks]
    )
    own.start()

    def out_copy(r):
        rows = pl.ds(r * BLK, BLK)
        return pltpu.make_async_copy(total.at[rows], future_hbm.at[rows], sems.at[r])

    for r in range(row_blocks):
        weights, at = (first_weights, r) if r < cut else (other_weights, r - cut)
        left = jnp.concatenate([weights[at, k] for k in range(slots)], axis=1)
        right = jnp.concatenate([whole[columns[0, r, k]] for k in range(slots)], axis=0)
        rows = pl.ds(r * BLK, BLK)
        added = jnp.dot(left, right, preferred_element_type=jnp.float32)
        total[rows, :] = shifted[rows, :].astype(jnp.float32) + added
        out_copy(r).start()
    own.wait()
    for r in range(row_blocks):
        out_copy(r).wait()


def product(columns, weights, shifted, pieces, halves):
    row_blocks = columns.shape[1]
    rows, width = shifted.shape
    return pl.pallas_call(
        functools.partial(product_kernel, halves),
        out_shape=[
            jax.ShapeDtypeStruct((row_blocks, BLK, width), jnp.bfloat16),
            jax.ShapeDtypeStruct((rows, width), jnp.float32),
        ],
        in_specs=[SMEM_SPEC] + [VMEM_SPEC] * (3 + len(pieces)),
        out_specs=[ANY_SPEC, ANY_SPEC],
        scratch_shapes=[
            pltpu.VMEM((halves * row_blocks, BLK, width), jnp.bfloat16),
            pltpu.VMEM((rows, width), jnp.float32),
            pltpu.SemaphoreType.DMA((row_blocks + 1,)),
        ],
        compiler_params=pltpu.CompilerParams(vmem_limit_bytes=40 << 20),
    )(columns, *weights, shifted, *pieces)


def per_device(excite, present_inverse, retarded, columns, future_in):
    delays, halves = lax.axis_size("delay"), lax.axis_size("row")
    planes = delays // PLANE
    rows, width = future_in.shape[1:]

    quarters = solve(excite, present_inverse, future_in)
    spread = [lax.ppermute(quarters[k], "delay", [(0, k)]) for k in (3, 2, 1)]
    narrowed = narrow(future_in)
    early_rows = columns.shape[1] // 4
    first_weights = fetch(retarded, 0, early_rows)
    spread[0], first_weights, narrowed = lax.optimization_barrier((spread[0], first_weights, narrowed))
    shifted = lax.ppermute(narrowed, "delay", [(i, i - 1) for i in range(1, delays)])
    piece = quarters[0] + spread[0] + spread[1] + spread[2]
    reach = planes
    while reach > 1:
        reach //= 2
        pairs = [
            (z * PLANE + q, (z + reach) * PLANE + q)
            for z in range(0, planes, 2 * reach)
            for q in range(PLANE)
        ]
        piece = piece + lax.ppermute(piece, "delay", pairs)
    other_weights = fetch(retarded, early_rows, columns.shape[1] - early_rows)
    piece, other_weights = lax.optimization_barrier((piece, other_weights))
    held = [piece] + [None] * (PLANE - 1)
    for mask in (3, 1, 2):
        held[mask] = lax.ppermute(piece, "delay", [(i, i ^ mask) for i in range(delays)])
    held[3], shifted = lax.optimization_barrier((held[3], shifted))
    pieces = list(held)
    for turn in range(1, halves):
        pairs = [(i, (i + turn) % halves) for i in range(halves)]
        pieces += [lax.ppermute(p, "row", pairs) for p in held]
    currents, future = product(
        columns, (first_weights, other_weights), shifted, pieces, halves
    )
    return currents.reshape(1, rows, width), future[None]


def solution(mesh):
    return jax.shard_map(
        per_device,
        mesh=mesh,
        in_specs=(
            P(None, "row", None),
            P("row", None, None),
            P("delay", "row", None, None, None),
            P("delay", "row", None),
            P("delay", "row", None),
        ),
        out_specs=(P(None, "row", None), P("delay", "row", None)),
        check_vma=False,
    )
```

```python
import functools

import jax
import jax.numpy as jnp
from jax import lax
from jax.experimental import pallas as pl
from jax.experimental.pallas import tpu as pltpu
from jax.sharding import PartitionSpec as P

BLK = 128
PLANE = 4

VMEM_SPEC = pl.BlockSpec(memory_space=pltpu.VMEM)
ANY_SPEC = pl.BlockSpec(memory_space=pl.ANY)
SMEM_SPEC = pl.BlockSpec(memory_space=pltpu.SMEM)


def solve_kernel(excite_hbm, inverse_hbm, future_hbm, *refs):
    quarters = refs[:PLANE]
    excite, inverse, future, sems = refs[PLANE:]
    step = quarters[0].shape[0]
    blocks = step // BLK
    root = lax.axis_index("delay") == 0

    def copies(part):
        rows = pl.ds(part * step, step)
        whole = pl.ds(part * blocks, blocks)
        return (
            pltpu.make_async_copy(future_hbm.at[0, rows], future.at[rows], sems.at[0, part]),
            pltpu.make_async_copy(excite_hbm.at[0, rows], excite.at[rows], sems.at[1, part]),
            pltpu.make_async_copy(inverse_hbm.at[whole], inverse.at[whole], sems.at[2, part]),
        )

    @pl.when(root)
    def _():
        for part in reversed(range(PLANE)):
            for copy in copies(part):
                copy.start()
        for part in reversed(range(PLANE)):
            for copy in copies(part):
                copy.wait()
            for block in range(blocks):
                rows = pl.ds(part * step + block * BLK, BLK)
                right = (excite[rows, :].astype(jnp.float32) - future[rows, :]).astype(jnp.bfloat16)
                solved = jnp.dot(
                    inverse[part * blocks + block], right, preferred_element_type=jnp.float32
                )
                quarters[part][pl.ds(block * BLK, BLK), :] = solved.astype(jnp.bfloat16)

    @pl.when(jnp.logical_not(root))
    def _():
        quarters[0][...] = jnp.zeros_like(quarters[0])


def solve(excite, inverse, future):
    rows, width = future.shape[1:]
    quarter = pltpu.VMEM((rows // PLANE, width), jnp.bfloat16)
    return pl.pallas_call(
        solve_kernel,
        out_shape=[quarter] * PLANE,
        in_specs=[ANY_SPEC] * 3,
        out_specs=[VMEM_SPEC] * PLANE,
        scratch_shapes=[
            pltpu.VMEM((rows, width), jnp.bfloat16),
            pltpu.VMEM(inverse.shape, jnp.bfloat16),
            pltpu.VMEM((rows, width), jnp.float32),
            pltpu.SemaphoreType.DMA((3, PLANE)),
        ],
    )(excite, inverse, future)


def narrow_kernel(parts, future_hbm, out, future, sems):
    step = future.shape[0] // parts

    def copy(part):
        rows = pl.ds(part * step, step)
        return pltpu.make_async_copy(future_hbm.at[0, rows], future.at[rows], sems.at[part])

    for part in range(parts):
        copy(part).start()
    for part in range(parts):
        copy(part).wait()
        rows = pl.ds(part * step, step)
        out[rows, :] = future[rows, :].astype(jnp.bfloat16)


def narrow(future):
    rows, width = future.shape[1:]
    return pl.pallas_call(
        functools.partial(narrow_kernel, PLANE),
        out_shape=pltpu.VMEM((rows, width), jnp.bfloat16),
        in_specs=[ANY_SPEC],
        out_specs=VMEM_SPEC,
        scratch_shapes=[
            pltpu.VMEM((rows, width), jnp.float32),
            pltpu.SemaphoreType.DMA((PLANE,)),
        ],
    )(future)


def fetch_kernel(first, weights_hbm, out, sem):
    copy = pltpu.make_async_copy(weights_hbm.at[0, pl.ds(first, out.shape[0])], out, sem)
    copy.start()
    copy.wait()


def fetch(weights, first, count):
    return pl.pallas_call(
        functools.partial(fetch_kernel, first),
        out_shape=jax.ShapeDtypeStruct((count,) + weights.shape[2:], weights.dtype),
        in_specs=[ANY_SPEC],
        out_specs=VMEM_SPEC,
        scratch_shapes=[pltpu.SemaphoreType.DMA],
        compiler_params=pltpu.CompilerParams(vmem_limit_bytes=40 << 20),
    )(pltpu.with_memory_space_constraint(weights, pltpu.HBM))


def product_kernel(halves, columns, first_weights, other_weights, shifted, *refs):
    pieces = refs[: halves * PLANE]
    currents_hbm, future_hbm, whole, total, sems = refs[halves * PLANE :]
    step = pieces[0].shape[0] // BLK
    row_blocks, slots = columns.shape[1:]
    cut = first_weights.shape[0]
    mine = lax.rem(lax.axis_index("delay"), PLANE)
    row = lax.axis_index("row")
    for turn in range(halves):
        half = lax.rem(row - turn + halves, halves)
        for mask in range(PLANE):
            start = (half * PLANE + lax.bitwise_xor(mine, mask)) * step
            piece = pieces[turn * PLANE + mask]
            for block in range(step):
                whole[start + block] = piece[pl.ds(block * BLK, BLK), :]

    own = pltpu.make_async_copy(
        whole.at[pl.ds(row * row_blocks, row_blocks)], currents_hbm, sems.at[row_blocks]
    )
    own.start()

    def out_copy(r):
        rows = pl.ds(r * BLK, BLK)
        return pltpu.make_async_copy(total.at[rows], future_hbm.at[rows], sems.at[r])

    for r in range(row_blocks):
        weights, at = (first_weights, r) if r < cut else (other_weights, r - cut)
        left = jnp.concatenate([weights[at, k] for k in range(slots)], axis=1)
        right = jnp.concatenate([whole[columns[0, r, k]] for k in range(slots)], axis=0)
        rows = pl.ds(r * BLK, BLK)
        added = jnp.dot(left, right, preferred_element_type=jnp.float32)
        total[rows, :] = shifted[rows, :].astype(jnp.float32) + added
        out_copy(r).start()
    own.wait()
    for r in range(row_blocks):
        out_copy(r).wait()


def product(columns, weights, shifted, pieces, halves):
    row_blocks = columns.shape[1]
    rows, width = shifted.shape
    return pl.pallas_call(
        functools.partial(product_kernel, halves),
        out_shape=[
            jax.ShapeDtypeStruct((row_blocks, BLK, width), jnp.bfloat16),
            jax.ShapeDtypeStruct((rows, width), jnp.float32),
        ],
        in_specs=[SMEM_SPEC] + [VMEM_SPEC] * (3 + len(pieces)),
        out_specs=[ANY_SPEC, ANY_SPEC],
        scratch_shapes=[
            pltpu.VMEM((halves * row_blocks, BLK, width), jnp.bfloat16),
            pltpu.VMEM((rows, width), jnp.float32),
            pltpu.SemaphoreType.DMA((row_blocks + 1,)),
        ],
        compiler_params=pltpu.CompilerParams(vmem_limit_bytes=40 << 20),
    )(columns, *weights, shifted, *pieces)


def per_device(excite, present_inverse, retarded, columns, future_in):
    delays, halves = lax.axis_size("delay"), lax.axis_size("row")
    planes = delays // PLANE
    rows, width = future_in.shape[1:]

    quarters = solve(excite, present_inverse, future_in)
    spread = [lax.ppermute(quarters[k], "delay", [(0, k)]) for k in (3, 2, 1)]
    narrowed = narrow(future_in)
    early_rows = columns.shape[1] // 4
    first_weights = fetch(retarded, 0, early_rows)
    spread[0], first_weights, narrowed = lax.optimization_barrier((spread[0], first_weights, narrowed))
    shifted = lax.ppermute(narrowed, "delay", [(i, i - 1) for i in range(1, delays)])
    piece = quarters[0] + spread[0] + spread[1] + spread[2]
    reach = planes
    while reach > 1:
        reach //= 2
        pairs = [
            (z * PLANE + q, (z + reach) * PLANE + q)
            for z in range(0, planes, 2 * reach)
            for q in range(PLANE)
        ]
        piece = piece + lax.ppermute(piece, "delay", pairs)
    other_weights = fetch(retarded, early_rows, columns.shape[1] - early_rows)
    piece, other_weights = lax.optimization_barrier((piece, other_weights))
    held = [piece] + [None] * (PLANE - 1)
    for mask in (3, 1, 2):
        held[mask] = lax.ppermute(piece, "delay", [(i, i ^ mask) for i in range(delays)])
    held[1], shifted = lax.optimization_barrier((held[1], shifted))
    pieces = list(held)
    for turn in range(1, halves):
        pairs = [(i, (i + turn) % halves) for i in range(halves)]
        pieces += [lax.ppermute(p, "row", pairs) for p in held]
    currents, future = product(
        columns, (first_weights, other_weights), shifted, pieces, halves
    )
    return currents.reshape(1, rows, width), future[None]


def solution(mesh):
    return jax.shard_map(
        per_device,
        mesh=mesh,
        in_specs=(
            P(None, "row", None),
            P("row", None, None),
            P("delay", "row", None, None, None),
            P("delay", "row", None),
            P("delay", "row", None),
        ),
        out_specs=(P(None, "row", None), P("delay", "row", None)),
        check_vma=False,
    )
```
